256 devices in a mesh: dp: 256 (over x, y, z, core).
Axes of the slice: x: 4, y: 4, z: 8, core: 2. Of those that a mesh axis runs over, the one named last changes fastest.
Arguments:
- queries: bfloat16 [256, 4096], P('dp'), may hold values from -8 to 8
- passages: bfloat16 [8192, 4096], P('dp'), may hold values from -16 to 16
- positives: int32 [256], replicated, may hold values from 0 to 8160, as said below
- hidden: bfloat16 [256, 256, 4096], P('dp'), may hold values from -6 to 6
- gain_attn: float32 [4096], replicated, may hold values from 0.25 to 1.75
- value_weight: bfloat16 [4096, 1024], replicated, may hold values from -0.09375 to 0.09375
- keys: bfloat16 [256, 256, 1024], P('dp'), may hold values from -6 to 6
- last_query: bfloat16 [256, 4096], P('dp'), may hold values from -160 to 160
- lengths: int32 [256], P('dp'), may hold values from 1 to 256
- gain_final: float32 [4096], replicated, may hold values from 0.25 to 1.75
Outputs:
- mean_loss: float32 [], replicated
- query_grad: float32 [256, 4096], P('dp')
- passage_grad: float32 [8192, 4096], P('dp')
- value_weight_grad: float32 [4096, 1024], P('dp')
- hidden_grad: bfloat16 [256, 256, 4096], P('dp')
The draws below stay inside these ranges and needn't reach their ends.
Inputs may be any that keep to these rules, and one draw needn't show every extreme that they name: `positives`: each query's positive is the first of some device's 32 passages (its index is a multiple of 32).
All inputs are finite; a program needn't handle non-finite values.
Results may differ from the reference program's by a relative error of at most 0.012.
Values may be sent and summed in bfloat16 or wider, within the bound.
A program may use at most 128 MiB of HBM per device.

```python
import math
import jax
import jax.numpy as jnp
from jax import lax

D = 4096
HEADS = 32
KV_HEADS = 8
HEAD_DIM = 128
PDEV = 32
WIN = 1
SEQ = 256
KV_WIDTH = 1024
NQ = 256
NP = 8192
WIN_ALL = 256
N_DP = 256


def shared_rows(key):
    pick_key, base_key = jax.random.split(key)
    window_count = WIN * (NP // PDEV)
    window_pick = jax.random.randint(pick_key, (NQ,), 0, window_count)
    window_pick = window_pick.at[0].set(0)
    window_pick = window_pick.at[NQ - 1].set(window_count - 1)
    targets = window_pick // WIN * PDEV + window_pick % WIN
    basis = jax.random.normal(base_key, (NP, D), jnp.float32)
    return (targets.astype(jnp.int32), basis)


def shared_keys(key):
    return jax.random.normal(jax.random.fold_in(key, 11), (WIN * (NP // PDEV), SEQ, KV_HEADS * HEAD_DIM), jnp.float32)


def draw_positives(key, part):
    targets, basis = shared_rows(key)
    return targets


def draw_passages(key, part):
    targets, basis = shared_rows(key)
    return jnp.clip(basis, -6.0, 6.0).astype(jnp.bfloat16)


def draw_queries(key, part):
    targets, basis = shared_rows(key)
    key = jax.random.fold_in(key, 5)
    noise = jax.random.normal(key, (NQ, D), jnp.float32)
    return jnp.clip(0.2 * basis[targets] + noise, -8.0, 8.0).astype(jnp.bfloat16)


def draw_keys(key, part):
    basis = shared_keys(key)
    return jnp.clip(basis, -6.0, 6.0).astype(jnp.bfloat16)


def draw_last_query(key, part):
    basis = jnp.clip(shared_keys(key), -6.0, 6.0)
    key = jax.random.fold_in(key, 9)
    count = basis.shape[0]
    drawn = jnp.clip(jax.random.normal(key, (count, D), jnp.float32), -6.0, 6.0)
    return jnp.clip(drawn, -160.0, 160.0).astype(jnp.bfloat16)


def set_ends(entries, rng, smallest, top_value):
    shape = entries.shape
    spot = [jax.random.randint(jax.random.fold_in(rng, axis), (), 0, shape[axis]) for axis in range(len(shape))]
    entries = entries.at[tuple(spot)].set(smallest)
    longest = shape.index(max(shape))
    spot[longest] = (spot[longest] + 1) % shape[longest]
    return entries.at[tuple(spot)].set(top_value)


def steps_of(own_key, extent, cuts, low, top_value):
    gain, own = 1.0, jax.random.fold_in(own_key, 6)
    for dim, blocks in cuts:
        heights = jnp.exp(jax.random.uniform(jax.random.fold_in(own, dim), (blocks,), jnp.float32, low / len(cuts), top_value / len(cuts)))
        gain = gain * jnp.repeat(heights, extent[dim] // blocks).reshape([-1 if axis == dim else 1 for axis in range(len(extent))])
    return gain


def gaussian(rng, dims, scale, reach, shards=(), held_as=jnp.bfloat16):
    result = jax.random.normal(rng, dims, jnp.float32) * scale
    if len(shards) > 0:
        result = steps_of(rng, dims, shards, -0.22, 0.18) * result
    return jnp.clip(result, min=-reach, max=reach).astype(held_as)


def setup_inputs(seed: int = 0) -> dict:
    streams_of = jax.random.split(jax.random.key(seed), 11)
    return {
        "queries": draw_queries(jax.random.fold_in(streams_of[10], 71), 0),
        "passages": draw_passages(jax.random.fold_in(streams_of[10], 71), 0),
        "positives": draw_positives(jax.random.fold_in(streams_of[10], 71), 0),
        "hidden": gaussian(streams_of[3], (WIN_ALL, SEQ, D), 1.0, 6.0, ((0, 256),)),
        "gain_attn": jnp.clip(1.0 + 0.15 * jax.random.normal(streams_of[4], (D,), jnp.float32), 0.25, 1.75),
        "value_weight": gaussian(streams_of[5], (D, KV_WIDTH), D ** -0.5, 0.09375),
        "keys": draw_keys(jax.random.fold_in(streams_of[10], 71), 0),
        "last_query": draw_last_query(jax.random.fold_in(streams_of[10], 71), 0),
        "lengths": set_ends(jax.random.randint(streams_of[8], (WIN_ALL,), 1, SEQ + 1), jax.random.fold_in(streams_of[8], 1), 1, SEQ).astype(jnp.int32),
        "gain_final": jnp.clip(1.0 + 0.15 * jax.random.normal(streams_of[9], (D,), jnp.float32), 0.25, 1.75),
    }


def unit_rows(matrix):
    divisor = jnp.sqrt(lax.optimization_barrier(jnp.sum(matrix * matrix, axis=1)) + 1e-06)
    return (matrix / divisor[:, None], divisor)

def tangent(gradient, unit, divisor):
    return (gradient - unit * lax.optimization_barrier(jnp.sum(unit * gradient, axis=1, keepdims=True))) / divisor[:, None]

def window(hidden, gain_attn, value_weight, keys, last_query, lengths, demb, gain_final):
    count, seq_len, width = hidden.shape
    kv_width = value_weight.shape[1]
    groups = HEADS // KV_HEADS
    hidden_wide = hidden.astype(jnp.float32)
    rscale = lax.rsqrt(lax.optimization_barrier(jnp.mean(hidden_wide * hidden_wide, axis=-1)) + 1e-05)
    normed = (hidden_wide * rscale[..., None] * gain_attn.astype(jnp.float32)).astype(jnp.bfloat16)
    flat_normed = normed.reshape(count * seq_len, width)
    values = jnp.dot(flat_normed, value_weight, preferred_element_type=jnp.float32).astype(jnp.bfloat16)
    query_heads = last_query.astype(jnp.float32).reshape(count, KV_HEADS, groups, HEAD_DIM)
    key_heads = keys.astype(jnp.float32).reshape(count, seq_len, KV_HEADS, HEAD_DIM)
    logits = jnp.einsum('bkgd,btkd->bkgt', query_heads, key_heads) / math.sqrt(HEAD_DIM)
    positions = jnp.arange(seq_len, dtype=jnp.int32)
    visible = positions[None, :] < lengths[:, None]
    logits = jnp.where(visible[:, None, None, :], logits, -1e+30)
    row_peak = lax.optimization_barrier(jnp.max(logits, axis=-1, keepdims=True))
    weights = jnp.exp(logits - row_peak)
    weights = weights / lax.optimization_barrier(jnp.sum(weights, axis=-1, keepdims=True))
    value_heads = values.astype(jnp.float32).reshape(count, seq_len, KV_HEADS, HEAD_DIM)
    context = jnp.einsum('bkgt,btkd->bkgd', weights, value_heads).reshape(count, width)
    last_pick = (positions[None, :] == lengths[:, None] - 1).astype(jnp.float32)
    final_in = jnp.einsum('bt,btd->bd', last_pick, hidden_wide)
    final_state = final_in + context
    oscale = lax.rsqrt(lax.optimization_barrier(jnp.mean(final_state * final_state, axis=-1)) + 1e-05)
    upstream = demb * gain_final.astype(jnp.float32)
    dstate = oscale[:, None] * (upstream - final_state * (oscale ** 2)[:, None] * lax.optimization_barrier(jnp.mean(upstream * final_state, axis=-1, keepdims=True)))
    dcontext = dstate.reshape(count, KV_HEADS, groups, HEAD_DIM)
    dvalues_full = jnp.einsum('bkgt,bkgd->btkd', weights, dcontext).reshape(count * seq_len, kv_width)
    dvalues = dvalues_full.astype(jnp.bfloat16)
    dnormed = jnp.dot(dvalues, value_weight.T, preferred_element_type=jnp.float32).reshape(count, seq_len, width)
    inner_grad = dnormed * gain_attn.astype(jnp.float32)
    input_grad = rscale[..., None] * (inner_grad - hidden_wide * (rscale ** 2)[..., None] * lax.optimization_barrier(jnp.mean(inner_grad * hidden_wide, axis=-1, keepdims=True)))
    input_grad = input_grad + last_pick[..., None] * dstate[:, None, :]
    return (input_grad.astype(jnp.bfloat16), flat_normed, dvalues_full)

def reference(queries, passages, positives, hidden, gain_attn, value_weight, keys, last_query, lengths, gain_final):
    precise = lax.Precision.HIGHEST
    q_unit, q_norm = unit_rows(queries.astype(jnp.float32))
    p_unit, p_norm = unit_rows(passages.astype(jnp.float32))
    scores = 50.0 * jnp.dot(q_unit, p_unit.T, precision=precise)
    expo_terms = jnp.exp(scores - 50.0)
    totals = lax.optimization_barrier(jnp.sum(expo_terms, axis=1))
    target = (positives[:, None] == jnp.arange(NP, dtype=jnp.int32)[None, :]).astype(jnp.float32)
    positive_hits = lax.optimization_barrier(jnp.sum(target * scores, axis=1))
    mean_loss = jnp.mean(jnp.log(totals) + 50.0 - positive_hits)
    coefficient = 50.0 * (expo_terms / totals[:, None] - target)
    query_sum = jnp.dot(coefficient, p_unit, precision=precise)
    passage_sum = jnp.dot(coefficient.T, q_unit, precision=precise)
    query_grad = tangent(query_sum, q_unit, q_norm)
    passage_grad = tangent(passage_sum, p_unit, p_norm)
    chosen = passage_grad.reshape(N_DP, PDEV, D)[:, :WIN]
    slabs = (hidden.reshape(N_DP, WIN, SEQ, D), keys.reshape(N_DP, WIN, SEQ, KV_WIDTH), last_query.reshape(N_DP, WIN, D), lengths.reshape(N_DP, WIN), chosen)

    def device_step(running, slab):
        grads, flat_normed, dvalues_full = window(slab[0], gain_attn, value_weight, slab[1], slab[2], slab[3], slab[4], gain_final)
        weight_term = lax.dot_general(flat_normed.astype(jnp.float32), dvalues_full, (((0,), (0,)), ((), ())), precision=precise, preferred_element_type=jnp.float32)
        return (running + weight_term, grads)
    weight_total, hidden_grads = lax.scan(device_step, jnp.zeros((D, KV_WIDTH), jnp.float32), slabs)
    return (mean_loss, query_grad, passage_grad, weight_total, hidden_grads.reshape(WIN_ALL, SEQ, D))
```

```python
import math

import jax
import jax.numpy as jnp
from jax import lax
from jax.experimental import pallas as pl
from jax.experimental.pallas import tpu as pltpu
from jax.sharding import PartitionSpec as P

HEADS = 32
KV_HEADS = 8
HEAD_DIM = 128
D = 4096
HALF = 2048
QCOL = 1024
BCOL = QCOL + 128
SEQ = 256
KVW = 1024
F32 = jnp.float32
BF16 = jnp.bfloat16
MESH = pl.DeviceIdType.MESH


def dot(a, b, ca, cb):
    return lax.dot_general(a, b, (((ca,), (cb,)), ((), ())), preferred_element_type=F32)


def total(v):
    return jnp.sum(jnp.sum(v, axis=1, keepdims=True), axis=0, keepdims=True)


def kernel(
    lengths, queries, passages, positives, hidden, gain_attn, value_weight, keys, last_query, gain_final,
    loss_out, query_out, passage_out, weight_out, hidden_out,
    len_in, q_in, p_all, pos_in, h_in, ga_in, wv_in, k_in, lq_in, gf_in,
    perm, rows32, q_rows, q_half, q_recv, q_a, q_b, s_own, s_all,
    tot_own, tot_a, tot_b, pool_own, pool_recv, pool_t, pool_rows, lhs_all, rhs_all, w_send, w_recv,
    wts, hcol, pg, spread, drow, hg, pool_rows32, wts_t,
    v1, va1, vb1, v_fwd, v2a, v2b, va2, vb2, v3, v3_recv, wg, qg,
    in_sem, out_sem, grp_send, grp_recv, one_send, one_recv, loc_sem,
):
    me = lax.axis_index("dp")
    g, i = me // 16, me % 16
    x, y, core = g // 4, g % 4, i % 2
    other = 1 - core
    sibling = g * 16 + (i + 1 - 2 * core)

    def grp_dev(j):
        return g * 16 + lax.rem(i + j, 16)

    def z_dev(j):
        return g * 16 + lax.rem(i + 2 * j, 16)

    def xy_dev(j):
        return lax.rem(g + j, 16) * 16 + i

    def x_dev(j):
        return (lax.rem(x + j, 4) * 4 + y) * 16 + i

    def y_dev(j):
        return (x * 4 + lax.rem(y + j, 4)) * 16 + i

    loads = []
    for n, (src, dst) in enumerate(
        (
            (queries, q_in), (lengths, len_in), (last_query, lq_in), (keys, k_in), (passages, p_all.at[core]), (hidden, h_in),
            (value_weight, wv_in), (positives, pos_in), (gain_attn, ga_in), (gain_final, gf_in),
        )
    ):
        copy = pltpu.make_async_copy(src, dst, in_sem.at[n])
        copy.start()
        loads.append(copy)
    l_query, l_len, l_last, l_keys, l_pass, l_hidden, l_value, l_pos, l_ga, l_gf = loads

    barrier = pltpu.get_barrier_semaphore()

    def greet(j, _):
        pl.semaphore_signal(barrier, inc=1, device_id=(grp_dev(j),), device_id_type=MESH)
        pl.semaphore_signal(barrier, inc=1, device_id=(xy_dev(j),), device_id_type=MESH)
        return 0

    lax.fori_loop(1, 16, greet, 0, unroll=True)

    def x_far(j):
        return x_dev(j) + 1 - 2 * core

    for j in range(1, 4):
        pl.semaphore_signal(barrier, inc=1, device_id=(x_far(j),), device_id_type=MESH)

    sends = []

    def send(src, dst, n, dev):
        copy = pltpu.make_async_remote_copy(
            src_ref=src, dst_ref=dst, send_sem=one_send.at[n], recv_sem=one_recv.at[n],
            device_id=(dev,), device_id_type=MESH,
        )
        copy.start()
        sends.append(copy)

    def arrived(ref, n):
        pltpu.make_async_remote_copy(
            src_ref=ref, dst_ref=ref, send_sem=one_send.at[n], recv_sem=one_recv.at[n],
            device_id=(sibling,), device_id_type=MESH,
        ).wait_recv()

    sprays = []

    def spray(n, device, src_of, dst_of, whole, stop=16):
        def step(j, _):
            pltpu.make_async_remote_copy(
                src_ref=src_of(j), dst_ref=dst_of(j), send_sem=grp_send.at[n], recv_sem=grp_recv.at[n],
                device_id=(device(j),), device_id_type=MESH,
            ).start()
            return 0

        lax.fori_loop(1, stop, step, 0, unroll=True)
        pltpu.make_async_copy(src_of(0), dst_of(0), grp_recv.at[n]).start()
        some = whole.at[pl.ds(0, stop - 1)]
        sprays.append(pltpu.make_async_copy(some, some, grp_send.at[n]))
        return pltpu.make_async_copy(whole, whole, grp_recv.at[n])

    l_query.wait()
    for r in range(32):
        q_rows[r : r + 1, :] = q_in[0:1, r * 128 : (r + 1) * 128].astype(F32)
    q_half[0] = q_rows[0:16, :].astype(BF16)
    q_half[1] = q_rows[16:32, :].astype(BF16)
    row = lax.broadcasted_iota(jnp.int32, (256, 256), 0)
    col = lax.broadcasted_iota(jnp.int32, (256, 256), 1)
    swap = ((row >> 4) == (col & 15)) & ((row & 15) == (col >> 4))
    perm[...] = jnp.where(swap, 1.0, 0.0).astype(BF16)

    pl.semaphore_wait(barrier, 33)

    q_came = spray(0, grp_dev, lambda j: q_half.at[lax.rem(i + j, 2)], lambda j: q_recv.at[i], q_recv)

    l_pass.wait()
    send(p_all.at[core], p_all.at[core], 52, sibling)

    l_last.wait()
    for r in range(32):
        rows32[r : r + 1, :] = lq_in[0:1, r * 128 : (r + 1) * 128].astype(F32)
    head = lax.broadcasted_iota(jnp.int32, (HEADS, KVW), 0) >> 2
    kv = lax.broadcasted_iota(jnp.int32, (HEADS, KVW), 1) >> 7
    same_kv = head == kv
    lq = rows32[...]
    query_wide = jnp.where(same_kv, jnp.concatenate([lq] * KV_HEADS, axis=1), 0.0).astype(BF16)
    l_keys.wait()
    logits = dot(query_wide, k_in[...], 1, 1) * (1.0 / math.sqrt(HEAD_DIM))
    token = lax.broadcasted_iota(jnp.int32, (HEADS, SEQ), 1)
    l_len.wait()
    count = len_in[0]
    logits = jnp.where(token < count, logits, -1e30)
    weights = jnp.exp(logits - jnp.max(logits, axis=1, keepdims=True))
    weights = weights / jnp.sum(weights, axis=1, keepdims=True)
    pick = jnp.where(lax.broadcasted_iota(jnp.int32, (16, SEQ), 1) == count - 1, 1.0, 0.0)
    pick = jnp.where(lax.broadcasted_iota(jnp.int32, (16, SEQ), 0) == 0, pick, 0.0)

    q_came.wait()
    turned = dot(perm[...], q_recv[...].reshape(256, 128), 1, 0)
    square = jnp.zeros((16, 128), F32)
    for j in range(16):
        part = turned[j * 16 : (j + 1) * 16, :]
        square = square + part * part
        part = part.astype(BF16)
        if j < 8:
            q_a[core, x, y, :, j * 128 : (j + 1) * 128] = part
        else:
            q_b[core, x, y, :, (j - 8) * 128 : (j - 7) * 128] = part
    square = jnp.broadcast_to(jnp.sum(square, axis=1, keepdims=True), (16, 128))
    top = square.astype(BF16)
    mid = (square - top.astype(F32)).astype(BF16)
    low = square - top.astype(F32) - mid.astype(F32)
    lane = lax.broadcasted_iota(jnp.int32, (16, 128), 1)
    ext = jnp.where(lane == 0, top.astype(F32), jnp.where(lane == 1, mid.astype(F32), jnp.where(lane == 2, low, 0.0)))
    q_b[core, x, y, :, QCOL:BCOL] = ext.astype(BF16)

    low, high, every = pl.ds(0, 2), pl.ds(2, 2), slice(None)

    def rest_of(order, h, near, part=every):
        return q_a.at[h, near, part] if order == 0 else q_b.at[h, part, near]

    def here(order):
        return x if order == 0 else y

    def along(order, j):
        return x_dev(j) if order == 0 else y_dev(j)

    def pass_ref(ref, n, dev):
        send(ref, ref, n, dev)

    def q_block():
        for j in range(1, 4):
            pass_ref(q_a.at[core, x, y], j, y_dev(j))
            pass_ref(q_b.at[core, x, y], 4 + j, x_dev(j))

    def q_line():
        for j in range(1, 4):
            arrived(q_a.at[core, x, lax.rem(y + 4 - j, 4)], j)
            arrived(q_b.at[core, lax.rem(x + 4 - j, 4), y], 4 + j)
        for order in range(2):
            line = rest_of(order, core, here(order))
            pass_ref(line, 9 + 4 * order, along(order, 1))
            pass_ref(line, 11 + 4 * order, along(order, 3))
        for order in range(2):
            pass_ref(rest_of(order, core, here(order)), 16 + 4 * order, sibling)

    def q_pass():
        for side, part in ((1, low), (3, high)):
            for order in range(2):
                near = lax.rem(here(order) + 4 - side, 4)
                arrived(rest_of(order, core, near), 8 + 4 * order + side)
                pass_ref(rest_of(order, core, near, part), 8 + 4 * order + (2 if side == 1 else 0), along(order, side))
                pass_ref(rest_of(order, core, near), 16 + 4 * order + side, sibling)
        for side, part in ((1, low), (3, high)):
            for order in range(2):
                far = lax.rem(here(order) + 2, 4)
                arrived(rest_of(order, core, far, part), 8 + 4 * order + (2 if side == 1 else 0))
                pass_ref(rest_of(order, core, far, part), 18 + 4 * order if side == 1 else 40 + order, sibling)

    def q_finish():
        for order in range(2):
            for side in (0, 1, 3):
                arrived(rest_of(order, other, lax.rem(here(order) + 4 - side, 4)), 16 + 4 * order + side)
            far = lax.rem(here(order) + 2, 4)
            arrived(rest_of(order, other, far, low), 18 + 4 * order)
            arrived(rest_of(order, other, far, high), 40 + order)

    def q_block_of(h, order):
        return (q_b if order else q_a)[h, :, :, :, 0:QCOL].reshape(256, QCOL)

    q_block()

    l_hidden.wait()

    def norm_rows(b, _):
        rows = pl.ds(pl.multiple_of(b * 16, 16), 16)
        part = h_in[rows, :].astype(F32)
        hcol[rows, :] = jnp.broadcast_to(jnp.sum(part * part, axis=1, keepdims=True), (16, 128))
        return 0

    lax.fori_loop(0, 16, norm_rows, 0, unroll=True)
    rs_col = lax.rsqrt(hcol[...] * (1.0 / D) + 1e-05)
    rs_row = jnp.transpose(rs_col)[0:1, :]
    scaled = weights * rs_row
    wts[0:32, :] = scaled.astype(BF16)
    wts[32:48, :] = pick.astype(BF16)
    wts_t[...] = jnp.transpose(jnp.concatenate([scaled, pick, jnp.zeros((80, SEQ), F32)], axis=0))[:, 0:48].astype(BF16)

    q_line()

    l_ga.wait()
    for n in range(8):
        cols = slice(n * 512, (n + 1) * 512)
        both = dot(wts[...], h_in[:, cols], 1, 0)
        drow[:, cols] = both[32:48, :]
        pooled = (both[0:32, :] * ga_in[:, cols]).astype(BF16)
        pool_rows32[:, cols] = pooled
        for p in (2 * n, 2 * n + 1):
            piece = pooled[:, (p - 2 * n) * 256 : (p - 2 * n + 1) * 256]
            spot = slice((p // 4) * 256, (p // 4 + 1) * 256)
            pool_own[p % 4, 0, :, spot] = piece[0:16, :]
            pool_own[p % 4, 1, :, spot] = piece[16:32, :]
    l_value.wait()

    def context(n):
        cols = slice(n * 512, (n + 1) * 512)
        wide = jnp.where(same_kv[:, cols], dot(pool_rows32[...], wv_in[:, cols], 1, 0), 0.0)
        return (wide[:, 0:128] + wide[:, 128:256]) + (wide[:, 256:384] + wide[:, 384:512])

    final = context(0)

    arrived(p_all.at[other], 52)
    wide_p = p_all[...].reshape(64, D).astype(F32)
    p_norm = jnp.sqrt(jnp.sum(wide_p * wide_p, axis=1, keepdims=True) + 1e-06)

    q_pass()

    for j in range(1, 4):
        send(pool_own.at[lax.rem(y + j, 4)], pool_recv.at[y], 24 + j, y_dev(j))
    keep_pool = pltpu.make_async_copy(pool_own.at[y], pool_recv.at[y], one_recv.at[24])
    keep_pool.start()

    rhs_all[...] = jnp.zeros((2048, 256), BF16)

    q_finish()
    l_pos.wait()
    three = jnp.where(lax.broadcasted_iota(jnp.int32, (16, 128), 1) < 3, 1.0, 0.0).astype(BF16)
    dots = jnp.zeros((64, 256), F32)
    q_square = jnp.zeros((16, 256), F32)
    for h in range(2):
        for order in range(2):
            first = h * HALF + order * QCOL
            dots = dots + dot(
                p_all[:, :, first : first + QCOL].reshape(64, QCOL), q_block_of(h, order), 1, 1
            )
        q_square = q_square + dot(three, q_b[h, :, :, :, QCOL:BCOL].reshape(256, 128), 1, 1)
    q_norm = jnp.sqrt(q_square[0:1, :] + 1e-06)
    cosine = dots / (p_norm * q_norm)
    scores = 50.0 * cosine
    expo = jnp.exp(scores - 50.0)
    column = (me - core) * 32 + lax.broadcasted_iota(jnp.int32, (64, 256), 0)
    target = jnp.where(pos_in[...] == column, 1.0, 0.0)
    tot_own[0, :, 0:256] = jnp.sum(expo, axis=0, keepdims=True)
    tot_own[0, :, 256:512] = jnp.sum(target * scores, axis=0, keepdims=True)
    tot_came = spray(3, z_dev, lambda j: tot_own.at[0], lambda j: tot_a.at[i // 2], tot_a, 8)

    keep_pool.wait()
    for j in range(1, 4):
        arrived(pool_recv.at[lax.rem(y + 4 - j, 4)], 24 + j)
    for h in range(2):
        half_rows = [pool_recv[:, h, :, xp * 512 : (xp + 1) * 512].reshape(64, 512).astype(F32) for xp in range(2)]
        turned = jnp.transpose(jnp.concatenate(half_rows, axis=0)).astype(BF16)
        for xl in range(2):
            pool_t[h, :, xl] = turned[xl * 256 : (xl + 1) * 256, :].reshape(8, 32, 128)
    rows_came = spray(
        2, grp_dev,
        lambda j: pool_t.at[lax.rem(i + j, 2), lax.rem(i + j, 16) // 2], lambda j: pool_rows.at[i], pool_rows,
    )

    tot_came.wait()
    acc = tot_a[0]
    for s in range(1, 8):
        acc = acc + tot_a[s]
    tot_own[1] = acc
    tot_came = spray(4, xy_dev, lambda j: tot_own.at[1], lambda j: tot_b.at[g], tot_b)

    final = final + context(1)
    for r in range(32):
        rows32[r : r + 1, :] = drow[0:1, r * 128 : (r + 1) * 128]
    final = final + rows32[...]
    oscale = lax.rsqrt(total(final * final) * (1.0 / D) + 1e-05)
    inv_p = 1.0 / p_norm
    tot_came.wait()
    acc = tot_b[0]
    for s in range(1, 16):
        acc = acc + tot_b[s]
    totals = acc[:, 0:256]
    coeff = 50.0 * (expo / totals - target)

    def v1_part(order, j, part):
        to = lax.rem(here(order) + j, 4)
        return v1.at[0, to, part] if order == 0 else v1.at[1, part, to]

    def ring(order, side, n):
        return (vb1 if order else va1).at[n + (0 if side == 1 else 3)]

    def ring_sem(order, side, n):
        return (49 if side == 1 else 42) + n + (4 if order and side == 1 else 3 if order else 0)

    by_p = jnp.transpose(jnp.concatenate([coeff * inv_p, jnp.zeros((64, 256), F32)], axis=0))[:, 0:64].astype(BF16)
    for order in range(2):
        for n in range(2):
            cols = pl.ds(pl.multiple_of(core * HALF + (order * QCOL + n * 512), 512), 512)
            part = dot(by_p, p_all[:, :, cols].reshape(64, 512), 1, 0)
            v1[order, :, :, :, n * 512 : (n + 1) * 512] = part.astype(BF16).reshape(4, 4, 16, 512)
        for side, part, rest in ((1, low, high), (3, high, low)):
            send(v1_part(order, 2, part), ring(order, side, 0), ring_sem(order, side, 0), along(order, side))
            send(v1_part(order, side, rest), ring(order, side, 1), ring_sem(order, side, 1), along(order, side))

    def own_rows(rows):
        return jnp.where(core == 0, rows[0:32], rows[32:64])

    by_q = (own_rows(coeff) / q_norm).astype(BF16)
    radial = own_rows(jnp.sum(coeff * cosine, axis=1, keepdims=True) * inv_p)
    inv_own = own_rows(inv_p)
    for n in range(4):
        cols = slice(n * QCOL, (n + 1) * QCOL)
        p_sum = dot(by_q, q_block_of(n // 2, n % 2), 1, 0)
        pg[:, cols] = (p_sum - p_all[core, :, cols].astype(F32) * radial) * inv_own
    out_p = pltpu.make_async_copy(pg, passage_out, out_sem.at[0])
    out_p.start()

    for r in range(32):
        rows32[r : r + 1, :] = pg[0:1, r * 128 : (r + 1) * 128]
    l_gf.wait()
    upstream = rows32[...] * gf_in[...]
    mean_uf = total(upstream * final) * (1.0 / D)
    dstate = oscale * (upstream - final * (oscale * oscale) * mean_uf)
    s_own[0] = dstate[0:16, :].astype(BF16)
    s_own[1] = dstate[16:32, :].astype(BF16)
    s_came = spray(5, grp_dev, lambda j: s_own.at[lax.rem(i + j, 2)], lambda j: s_all.at[y, i], s_all.at[y])

    for order in range(2):
        for side, part in ((1, low), (3, high)):
            arrived(ring(order, side, 0), ring_sem(order, side, 0))
            added = v1_part(order, side, part)[...].astype(F32) + ring(order, side, 0)[...].astype(F32)
            slot = order * 2 + (0 if side == 1 else 1)
            v_fwd[slot] = added.astype(BF16)
            send(v_fwd.at[slot], ring(order, side, 2), ring_sem(order, side, 2), along(order, side))

    rows_came.wait()
    lane_kv = (lax.broadcasted_iota(jnp.int32, (64, 128), 1) & 15) >> 2
    for s in range(16):
        rows = pool_rows[s].reshape(64, 128).astype(F32)
        for k in range(4):
            lhs_all[k * 64 : (k + 1) * 64, s * 128 : (s + 1) * 128] = jnp.where(lane_kv == k, rows, 0.0).astype(BF16)

    s_came.wait()
    for j in range(1, 4):
        send(s_all.at[y], s_all.at[y], 28 + j, y_dev(j))

    dstate_wide = jnp.where(same_kv, jnp.concatenate([dstate] * KV_HEADS, axis=1), 0.0).astype(BF16)
    drow[...] = jnp.zeros((16, D), F32)
    for r in range(32):
        drow[0:1, r * 128 : (r + 1) * 128] = dstate[r : r + 1, :]
    spread[32:48, :] = drow[...].astype(BF16)
    for n in range(0, 4):
        cols = slice(n * 512, (n + 1) * 512)
        spread[0:32, cols] = (dot(dstate_wide, wv_in[cols, :], 1, 1) * ga_in[:, cols]).astype(BF16)

    sums = []
    for order in range(2):
        for side in (1, 3):
            for n in (1, 2):
                arrived(ring(order, side, n), ring_sem(order, side, n))
        for part, side in ((low, 1), (high, 3)):
            piece = v1_part(order, 0, part)[...].astype(F32)
            piece = piece + ring(order, side, 2)[...].astype(F32)
            sums.append(piece + ring(order, 4 - side, 1)[...].astype(F32))
    acc_a = jnp.concatenate(sums[0:2], axis=0)
    acc_b = jnp.concatenate(sums[2:4], axis=0)
    v2a[...] = acc_a.astype(BF16)
    v2b[...] = acc_b.astype(BF16)
    for j in range(1, 4):
        send(v2a.at[lax.rem(y + j, 4)], va2.at[j - 1], 56 + j, y_dev(j))
        send(v2b.at[lax.rem(x + j, 4)], vb2.at[j - 1], 60 + j, x_dev(j))

    for n in range(4, 8):
        cols = slice(n * 512, (n + 1) * 512)
        spread[0:32, cols] = (dot(dstate_wide, wv_in[cols, :], 1, 1) * ga_in[:, cols]).astype(BF16)

    for j in range(1, 4):
        arrived(s_all.at[lax.rem(y + 4 - j, 4)], 28 + j)
    for s in range(16):
        block = s_all[:, s].reshape(64, 128)
        rhs_all[s * 128 : s * 128 + 64, 0:128] = block
        rhs_all[s * 128 + 64 : (s + 1) * 128, 128:256] = block
    grads = dot(lhs_all[...], rhs_all[...], 1, 0).astype(BF16)
    for to in range(8):
        xp, xl, cr = to // 4, (to // 2) % 2, to % 2
        for k in range(4):
            first = k * 64 + xl * 32 + cr * 16
            w_send[xp * 2 + xl, cr, :, k * 128 : (k + 1) * 128] = grads[
                first : first + 16, xp * 128 : (xp + 1) * 128
            ]
    for j in range(1, 4):
        send(w_send.at[lax.rem(x + j, 4), core], w_recv.at[x, core], 32 + j, x_dev(j))
        send(w_send.at[lax.rem(x + j, 4), other], w_recv.at[x, core], 36 + j, x_far(j))
    send(w_send.at[x, other], w_recv.at[x, core], 36, sibling)
    keep_w = pltpu.make_async_copy(w_send.at[x, core], w_recv.at[x, core], one_recv.at[32])
    keep_w.start()

    for j in range(1, 4):
        arrived(va2.at[j - 1], 56 + j)
        arrived(vb2.at[j - 1], 60 + j)
    acc_a = v2a[y].astype(F32)
    acc_b = v2b[x].astype(F32)
    for j in range(3):
        acc_a = acc_a + va2[j].astype(F32)
        acc_b = acc_b + vb2[j].astype(F32)
    pieces = [acc_a[:, j * 128 : (j + 1) * 128] for j in range(8)]
    pieces += [acc_b[:, j * 128 : (j + 1) * 128] for j in range(8)]
    stacked = jnp.concatenate([piece.astype(BF16) for piece in pieces], axis=0)
    v3[...] = dot(perm[...], stacked, 1, 0).astype(BF16).reshape(16, 16, 128)
    v3_came = spray(6, grp_dev, lambda j: v3.at[lax.rem(i + j, 16)], lambda j: v3_recv.at[i], v3_recv)

    loss = total(jnp.log(totals) + 50.0 - acc[:, 256:512]) * (1.0 / 256.0)
    loss_out[...] = jnp.broadcast_to(loss, (1, 128))

    mix = dot(spread[0:32, :], h_in[...], 1, 1)
    mean_row = jnp.sum(weights * mix, axis=0, keepdims=True) * (rs_row * rs_row * rs_row) * (1.0 / D)
    mean_all = jnp.transpose(jnp.broadcast_to(mean_row, (128, 256)))


    def hidden_rows(b):
        rows = slice(b * 128, (b + 1) * 128)
        for n in range(8):
            cols = slice(n * 512, (n + 1) * 512)
            grad = dot(wts_t[rows, :], spread[:, cols], 1, 0)
            scale = jnp.concatenate([mean_all[rows]] * 4, axis=1)
            hg[b, :, cols] = (grad - h_in[rows, cols].astype(F32) * scale).astype(BF16)
        copy = pltpu.make_async_copy(hg.at[b], hidden_out.at[pl.ds(b * 128, 128)], out_sem.at[1 + b])
        copy.start()
        return copy

    out_h = [hidden_rows(0), hidden_rows(1)]

    keep_w.wait()
    arrived(w_recv.at[x, other], 36)
    for j in range(1, 4):
        arrived(w_recv.at[lax.rem(x + 4 - j, 4), core], 32 + j)
        arrived(w_recv.at[lax.rem(x + 4 - j, 4), other], 36 + j)
    for h in range(2):
        acc_w = w_recv[0, h].astype(F32)
        for s in range(1, 4):
            acc_w = acc_w + w_recv[s, h].astype(F32)
        wg[:, h * 512 : (h + 1) * 512] = acc_w
    out_w = pltpu.make_async_copy(wg, weight_out, out_sem.at[3])
    out_w.start()

    for copy in sends:
        copy.wait_send()
    for wait in sprays:
        wait.wait()
    out_p.wait()
    for copy in out_h:
        copy.wait()
    out_w.wait()

    v3_came.wait()
    halves = []
    for h in range(2):
        acc_q = v3_recv[h].astype(F32)
        for s in range(1, 8):
            acc_q = acc_q + v3_recv[2 * s + h].astype(F32)
        halves.append(acc_q)
    q_sum = jnp.concatenate(halves, axis=0)
    own = q_rows[...]
    own_square = total(own * own) + 1e-06
    own_dot = total(own * q_sum)
    qg[...] = (q_sum - own * (own_dot / own_square)) * lax.rsqrt(own_square)
    out_q = pltpu.make_async_copy(qg, query_out, out_sem.at[4])
    out_q.start()
    out_q.wait()


def hand_on(
    l_in, q_in, p_in, w_in, h_in, l_out, q_out, p_out, w_out, h_out, l_via, q_via, p_via, w_via, h_via, sem_in, sem_out
):
    steps = [(l_in, l_via, l_out), (q_in, q_via, q_out), (w_in, w_via, w_out), (p_in, p_via, p_out)]
    for n in range(4):
        rows = pl.ds(n * 64, 64)
        steps.append((h_in.at[rows], h_via.at[rows], h_out.at[rows]))
    loads = [pltpu.make_async_copy(src, via, sem_in.at[n]) for n, (src, via, _) in enumerate(steps)]
    stores = [pltpu.make_async_copy(via, dst, sem_out.at[n]) for n, (_, via, dst) in enumerate(steps)]
    for load in loads:
        load.start()
    for load, store in zip(loads, stores):
        load.wait()
        store.start()
    for store in stores:
        store.wait()


def per_device(
    queries, passages, positives, hidden, gain_attn, value_weight, keys, last_query, lengths, gain_final
):
    anywhere = pl.BlockSpec(memory_space=pl.ANY)
    vmem = pltpu.VMEM
    dma = pltpu.SemaphoreType.DMA
    scratch = [
        pltpu.SMEM((1,), jnp.int32), vmem((1, D), BF16), vmem((2, 32, D), BF16), vmem((1, 256), jnp.int32), vmem((SEQ, D), BF16),
        vmem((1, D), F32), vmem((D, KVW), BF16), vmem((SEQ, KVW), BF16), vmem((1, D), BF16),
        vmem((32, 128), F32),
        vmem((256, 256), BF16), vmem((32, 128), F32), vmem((32, 128), F32), vmem((2, 16, 128), BF16),
        vmem((16, 16, 128), BF16), vmem((2, 4, 4, 16, QCOL), BF16), vmem((2, 4, 4, 16, BCOL), BF16), vmem((2, 16, 128), BF16),
        vmem((4, 16, 16, 128), BF16),
        vmem((2, 1, 512), F32), vmem((8, 1, 512), F32), vmem((16, 1, 512), F32), vmem((4, 2, 16, 1024), BF16),
        vmem((4, 2, 16, 1024), BF16), vmem((2, 8, 2, 32, 128), BF16), vmem((16, 2, 32, 128), BF16),
        vmem((256, 2048), BF16), vmem((2048, 256), BF16), vmem((4, 2, 16, 512), BF16), vmem((4, 2, 16, 512), BF16),
        vmem((48, SEQ), BF16), vmem((SEQ, 128), F32), vmem((32, D), F32), vmem((48, D), BF16),
        vmem((16, D), F32), vmem((2, 128, D), BF16),
        vmem((32, D), BF16), vmem((SEQ, 48), BF16),
        vmem((2, 4, 4, 16, QCOL), BF16), vmem((6, 2, 16, QCOL), BF16), vmem((6, 2, 16, QCOL), BF16),
        vmem((4, 2, 16, QCOL), BF16),
        vmem((4, 16, QCOL), BF16), vmem((4, 16, QCOL), BF16), vmem((3, 16, QCOL), BF16),
        vmem((3, 16, QCOL), BF16), vmem((16, 16, 128), BF16), vmem((16, 16, 128), BF16),
        vmem((16, KVW), F32), vmem((32, 128), F32),
        dma((10,)), dma((5,)), dma((7,)), dma((7,)), dma((64,)), dma((64,)), dma((1,)),
    ]
    loss, query_grad, passage_grad, weight_grad, hidden_grad = pl.pallas_call(
        kernel,
        out_shape=(
            jax.ShapeDtypeStruct((1, 128), F32),
            jax.ShapeDtypeStruct((32, 128), F32),
            jax.ShapeDtypeStruct((32, D), F32),
            jax.ShapeDtypeStruct((16, KVW), F32),
            jax.ShapeDtypeStruct((SEQ, D), BF16),
        ),
        in_specs=[anywhere] * 10,
        out_specs=(pl.BlockSpec(memory_space=pltpu.VMEM),) + (anywhere,) * 4,
        scratch_shapes=scratch,
        compiler_params=pltpu.CompilerParams(
            collective_id=0, has_side_effects=True, vmem_limit_bytes=56 * 1024 * 1024
        ),
    )(
        lengths, queries, passages, positives.reshape(1, 256), hidden.reshape(SEQ, D),
        gain_attn.reshape(1, D), value_weight, keys.reshape(SEQ, KVW), last_query,
        gain_final.reshape(32, 128),
    )
    grads = (loss, query_grad, passage_grad, weight_grad, hidden_grad)
    loss, query_grad, passage_grad, weight_grad, hidden_grad = pl.pallas_call(
        hand_on,
        out_shape=tuple(jax.ShapeDtypeStruct(leaf.shape, leaf.dtype) for leaf in grads),
        in_specs=[anywhere] * 5,
        out_specs=(anywhere,) * 5,
        scratch_shapes=[vmem(leaf.shape, leaf.dtype) for leaf in grads] + [dma((8,)), dma((8,))],
        compiler_params=pltpu.CompilerParams(vmem_limit_bytes=56 * 1024 * 1024),
    )(*grads)
    return (loss[0, 0], query_grad.reshape(1, D), passage_grad, weight_grad, hidden_grad.reshape(1, SEQ, D))


def solution(mesh):
    placed = (
        P("dp", None),
        P("dp", None),
        P(),
        P("dp", None, None),
        P(),
        P(),
        P("dp", None, None),
        P("dp", None),
        P("dp"),
        P(),
    )
    return jax.shard_map(
        per_device,
        mesh=mesh,
        in_specs=placed,
        out_specs=(P(), P("dp", None), P("dp", None), P("dp", None), P("dp", None, None)),
        check_vma=False,
    )
```

```python
import math

import jax
import jax.numpy as jnp
from jax import lax
from jax.experimental import pallas as pl
from jax.experimental.pallas import tpu as pltpu
from jax.sharding import PartitionSpec as P

HEADS = 32
KV_HEADS = 8
HEAD_DIM = 128
D = 4096
HALF = 2048
QCOL = 1024
BCOL = QCOL + 128
SEQ = 256
KVW = 1024
F32 = jnp.float32
BF16 = jnp.bfloat16
MESH = pl.DeviceIdType.MESH


def dot(a, b, ca, cb):
    return lax.dot_general(a, b, (((ca,), (cb,)), ((), ())), preferred_element_type=F32)


def total(v):
    return jnp.sum(jnp.sum(v, axis=1, keepdims=True), axis=0, keepdims=True)


def kernel(
    lengths, queries, passages, positives, hidden, gain_attn, value_weight, keys, last_query, gain_final,
    loss_out, query_out, passage_out, weight_out, hidden_out,
    len_in, q_in, p_all, pos_in, h_in, ga_in, wv_in, k_in, lq_in, gf_in,
    perm, rows32, q_rows, q_half, q_recv, q_a, q_b, s_own, s_all,
    tot_own, tot_a, tot_b, pool_own, pool_recv, pool_t, pool_rows, lhs_all, rhs_all, w_send, w_recv,
    wts, hcol, pg, spread, drow, hg, pool_rows32, wts_t, g_own, d_sib,
    v1, va1, vb1, v_fwd, v2a, v2b, va2, vb2, v3, v3_recv, wg, qg,
    in_sem, out_sem, grp_send, grp_recv, one_send, one_recv, loc_sem,
):
    me = lax.axis_index("dp")
    g, i = me // 16, me % 16
    x, y, core = g // 4, g % 4, i % 2
    other = 1 - core
    sibling = g * 16 + (i + 1 - 2 * core)

    def grp_dev(j):
        return g * 16 + lax.rem(i + j, 16)

    def z_dev(j):
        return g * 16 + lax.rem(i + 2 * j, 16)

    def xy_dev(j):
        return (lax.rem(x + j // 4, 4) * 4 + lax.rem(y + j % 4, 4)) * 16 + i

    def x_dev(j):
        return (lax.rem(x + j, 4) * 4 + y) * 16 + i

    def y_dev(j):
        return (x * 4 + lax.rem(y + j, 4)) * 16 + i

    def outward(k, mid):
        return mid + ((k + 1) // 2) * (1 - 2 * (k % 2))

    def outward_xy(k):
        return outward(k // 4, 2) * 4 + outward(k % 4, 2)

    l_query = pltpu.make_async_copy(queries, q_in, in_sem.at[0])
    l_query.start()

    barrier = pltpu.get_barrier_semaphore()

    def greet(k, _):
        pl.semaphore_signal(barrier, inc=1, device_id=(grp_dev(outward(k, 8)),), device_id_type=MESH)
        pl.semaphore_signal(barrier, inc=1, device_id=(xy_dev(outward_xy(k)),), device_id_type=MESH)
        return 0

    lax.fori_loop(0, 15, greet, 0, unroll=True)

    def x_far(j):
        return x_dev(j) + 1 - 2 * core

    for j in range(1, 4):
        pl.semaphore_signal(barrier, inc=1, device_id=(x_far(j),), device_id_type=MESH)

    loads = []
    for n, (src, dst) in enumerate(
        (
            (lengths, len_in), (last_query, lq_in), (keys, k_in), (passages, p_all.at[core]), (hidden, h_in),
            (value_weight, wv_in), (positives, pos_in), (gain_attn, ga_in), (gain_final, gf_in),
        )
    ):
        copy = pltpu.make_async_copy(src, dst, in_sem.at[n + 1])
        copy.start()
        loads.append(copy)
    l_len, l_last, l_keys, l_pass, l_hidden, l_value, l_pos, l_ga, l_gf = loads

    sends = []

    def send(src, dst, n, dev):
        copy = pltpu.make_async_remote_copy(
            src_ref=src, dst_ref=dst, send_sem=one_send.at[n], recv_sem=one_recv.at[n],
            device_id=(dev,), device_id_type=MESH,
        )
        copy.start()
        sends.append(copy)

    def arrived(ref, n):
        pltpu.make_async_remote_copy(
            src_ref=ref, dst_ref=ref, send_sem=one_send.at[n], recv_sem=one_recv.at[n],
            device_id=(sibling,), device_id_type=MESH,
        ).wait_recv()

    sprays = []

    def spray(n, device, src_of, dst_of, whole, stop=16):
        def step(k, _):
            j = outward_xy(k) if device is xy_dev else outward(k, stop // 2)
            pltpu.make_async_remote_copy(
                src_ref=src_of(j), dst_ref=dst_of(j), send_sem=grp_send.at[n], recv_sem=grp_recv.at[n],
                device_id=(device(j),), device_id_type=MESH,
            ).start()
            return 0

        lax.fori_loop(0, stop - 1, step, 0, unroll=True)
        pltpu.make_async_copy(src_of(0), dst_of(0), grp_recv.at[n]).start()
        some = whole.at[pl.ds(0, stop - 1)]
        sprays.append(pltpu.make_async_copy(some, some, grp_send.at[n]))
        return pltpu.make_async_copy(whole, whole, grp_recv.at[n])

    l_query.wait()
    for r in range(32):
        q_rows[r : r + 1, :] = q_in[0:1, r * 128 : (r + 1) * 128].astype(F32)
    q_half[0] = q_rows[0:16, :].astype(BF16)
    q_half[1] = q_rows[16:32, :].astype(BF16)
    row = lax.broadcasted_iota(jnp.int32, (256, 256), 0)
    col = lax.broadcasted_iota(jnp.int32, (256, 256), 1)
    swap = ((row >> 4) == (col & 15)) & ((row & 15) == (col >> 4))
    perm[...] = jnp.where(swap, 1.0, 0.0).astype(BF16)

    pl.semaphore_wait(barrier, 33)

    q_came = spray(0, grp_dev, lambda j: q_half.at[lax.rem(i + j, 2)], lambda j: q_recv.at[i], q_recv)

    l_pass.wait()
    send(p_all.at[core], p_all.at[core], 52, sibling)

    l_last.wait()
    for r in range(32):
        rows32[r : r + 1, :] = lq_in[0:1, r * 128 : (r + 1) * 128].astype(F32)
    head = lax.broadcasted_iota(jnp.int32, (HEADS, KVW), 0) >> 2
    kv = lax.broadcasted_iota(jnp.int32, (HEADS, KVW), 1) >> 7
    same_kv = head == kv
    lq = rows32[...]
    query_wide = jnp.where(same_kv, jnp.concatenate([lq] * KV_HEADS, axis=1), 0.0).astype(BF16)
    l_keys.wait()
    logits = dot(query_wide, k_in[...], 1, 1) * (1.0 / math.sqrt(HEAD_DIM))
    token = lax.broadcasted_iota(jnp.int32, (HEADS, SEQ), 1)
    l_len.wait()
    count = len_in[0]
    logits = jnp.where(token < count, logits, -1e30)
    weights = jnp.exp(logits - jnp.max(logits, axis=1, keepdims=True))
    weights = weights / jnp.sum(weights, axis=1, keepdims=True)
    pick = jnp.where(lax.broadcasted_iota(jnp.int32, (16, SEQ), 1) == count - 1, 1.0, 0.0)
    pick = jnp.where(lax.broadcasted_iota(jnp.int32, (16, SEQ), 0) == 0, pick, 0.0)

    q_came.wait()
    turned = dot(perm[...], q_recv[...].reshape(256, 128), 1, 0)
    square = jnp.zeros((16, 128), F32)
    for j in range(16):
        part = turned[j * 16 : (j + 1) * 16, :]
        square = square + part * part
        part = part.astype(BF16)
        if j < 8:
            q_a[core, x, y, :, j * 128 : (j + 1) * 128] = part
        else:
            q_b[core, x, y, :, (j - 8) * 128 : (j - 7) * 128] = part
    low, high, every = pl.ds(0, 2), pl.ds(2, 2), slice(None)

    def rest_of(order, h, near, part=every):
        return q_a.at[h, near, part] if order == 0 else q_b.at[h, part, near]

    def here(order):
        return x if order == 0 else y

    def along(order, j):
        return x_dev(j) if order == 0 else y_dev(j)

    def pass_ref(ref, n, dev):
        send(ref, ref, n, dev)


    def q_line():
        for j in range(1, 4):
            arrived(q_a.at[core, x, lax.rem(y + 4 - j, 4)], j)
            arrived(q_b.at[core, lax.rem(x + 4 - j, 4), y], 4 + j)
        for order in range(2):
            line = rest_of(order, core, here(order))
            pass_ref(line, 9 + 4 * order, along(order, 1))
            pass_ref(line, 11 + 4 * order, along(order, 3))
        for order in range(2):
            pass_ref(rest_of(order, core, here(order)), 16 + 4 * order, sibling)

    def q_pass():
        for side, part in ((1, low), (3, high)):
            for order in range(2):
                near = lax.rem(here(order) + 4 - side, 4)
                arrived(rest_of(order, core, near), 8 + 4 * order + side)
                pass_ref(rest_of(order, core, near, part), 8 + 4 * order + (2 if side == 1 else 0), along(order, side))
                pass_ref(rest_of(order, core, near), 16 + 4 * order + side, sibling)
    def q_rest():
        for side, part in ((1, low), (3, high)):
            for order in range(2):
                far = lax.rem(here(order) + 2, 4)
                arrived(rest_of(order, core, far, part), 8 + 4 * order + (2 if side == 1 else 0))
                pass_ref(rest_of(order, core, far, part), 18 + 4 * order if side == 1 else 40 + order, sibling)

    def q_finish():
        for order in range(2):
            for side in (0, 1, 3):
                arrived(rest_of(order, other, lax.rem(here(order) + 4 - side, 4)), 16 + 4 * order + side)
            far = lax.rem(here(order) + 2, 4)
            arrived(rest_of(order, other, far, low), 18 + 4 * order)
            arrived(rest_of(order, other, far, high), 40 + order)

    def q_block_of(h, order):
        return (q_b if order else q_a)[h, :, :, :, 0:QCOL].reshape(256, QCOL)

    for j in range(1, 4):
        pass_ref(q_a.at[core, x, y], j, y_dev(j))
    square = jnp.broadcast_to(jnp.sum(square, axis=1, keepdims=True), (16, 128))
    top = square.astype(BF16)
    mid = (square - top.astype(F32)).astype(BF16)
    bottom = square - top.astype(F32) - mid.astype(F32)
    lane = lax.broadcasted_iota(jnp.int32, (16, 128), 1)
    ext = jnp.where(lane == 0, top.astype(F32), jnp.where(lane == 1, mid.astype(F32), jnp.where(lane == 2, bottom, 0.0)))
    q_b[core, x, y, :, QCOL:BCOL] = ext.astype(BF16)
    for j in range(1, 4):
        pass_ref(q_b.at[core, x, y], 4 + j, x_dev(j))

    l_hidden.wait()

    def norm_rows(b, _):
        rows = pl.ds(pl.multiple_of(b * 16, 16), 16)
        part = h_in[rows, :].astype(F32)
        hcol[rows, :] = jnp.broadcast_to(jnp.sum(part * part, axis=1, keepdims=True), (16, 128))
        return 0

    lax.fori_loop(0, 16, norm_rows, 0, unroll=True)
    rs_col = lax.rsqrt(hcol[...] * (1.0 / D) + 1e-05)
    rs_row = jnp.transpose(rs_col)[0:1, :]
    scaled = weights * rs_row
    wts[0:32, :] = scaled.astype(BF16)
    wts[32:48, :] = pick.astype(BF16)
    wts_t[...] = jnp.transpose(jnp.concatenate([scaled, pick, jnp.zeros((80, SEQ), F32)], axis=0))[:, 0:48].astype(BF16)

    q_line()

    l_ga.wait()
    for n in range(8):
        cols = slice(n * 512, (n + 1) * 512)
        both = dot(wts[...], h_in[:, cols], 1, 0)
        drow[:, cols] = both[32:48, :]
        pooled = (both[0:32, :] * ga_in[:, cols]).astype(BF16)
        pool_rows32[:, cols] = pooled
        for p in (2 * n, 2 * n + 1):
            piece = pooled[:, (p - 2 * n) * 256 : (p - 2 * n + 1) * 256]
            spot = slice((p // 4) * 256, (p // 4 + 1) * 256)
            pool_own[p % 4, 0, :, spot] = piece[0:16, :]
            pool_own[p % 4, 1, :, spot] = piece[16:32, :]
    l_value.wait()

    def context(n):
        cols = slice(n * 512, (n + 1) * 512)
        wide = jnp.where(same_kv[:, cols], dot(pool_rows32[...], wv_in[:, cols], 1, 0), 0.0)
        return (wide[:, 0:128] + wide[:, 128:256]) + (wide[:, 256:384] + wide[:, 384:512])

    final = context(0)

    arrived(p_all.at[other], 52)
    wide_p = p_all[...].reshape(64, D).astype(F32)
    p_norm = jnp.sqrt(jnp.sum(wide_p * wide_p, axis=1, keepdims=True) + 1e-06)

    q_pass()

    for j in range(1, 4):
        send(pool_own.at[lax.rem(y + j, 4)], pool_recv.at[y], 24 + j, y_dev(j))
    keep_pool = pltpu.make_async_copy(pool_own.at[y], pool_recv.at[y], one_recv.at[24])
    keep_pool.start()

    final = final + context(1)
    for r in range(32):
        rows32[r : r + 1, :] = drow[0:1, r * 128 : (r + 1) * 128]
    final = final + rows32[...]
    oscale = lax.rsqrt(total(final * final) * (1.0 / D) + 1e-05)

    q_rest()

    l_pos.wait()
    three = jnp.where(lax.broadcasted_iota(jnp.int32, (16, 128), 1) < 3, 1.0, 0.0).astype(BF16)

    def half_scores(h):
        rows = jnp.zeros((64, 256), F32)
        for order in range(2):
            cols = pl.ds(pl.multiple_of(h * HALF + order * QCOL, QCOL), QCOL)
            rows = rows + dot(p_all[:, :, cols].reshape(64, QCOL), q_block_of(h, order), 1, 1)
        return rows, dot(three, q_b[h, :, :, :, QCOL:BCOL].reshape(256, 128), 1, 1)

    dots_here, square_here = half_scores(core)
    q_finish()
    dots_there, square_there = half_scores(other)
    dots = dots_here + dots_there
    q_square = square_here + square_there
    q_norm = jnp.sqrt(q_square[0:1, :] + 1e-06)
    cosine = dots / (p_norm * q_norm)
    scores = 50.0 * cosine
    expo = jnp.exp(scores - 50.0)
    column = (me - core) * 32 + lax.broadcasted_iota(jnp.int32, (64, 256), 0)
    target = jnp.where(pos_in[...] == column, 1.0, 0.0)
    tot_own[0, :, 0:256] = jnp.sum(expo, axis=0, keepdims=True)
    tot_own[0, :, 256:512] = jnp.sum(target * scores, axis=0, keepdims=True)
    tot_came = spray(3, z_dev, lambda j: tot_own.at[0], lambda j: tot_a.at[i // 2], tot_a, 8)

    keep_pool.wait()
    for j in range(1, 4):
        arrived(pool_recv.at[lax.rem(y + 4 - j, 4)], 24 + j)
    for h in range(2):
        half_rows = [pool_recv[:, h, :, xp * 512 : (xp + 1) * 512].reshape(64, 512).astype(F32) for xp in range(2)]
        turned = jnp.transpose(jnp.concatenate(half_rows, axis=0)).astype(BF16)
        for xl in range(2):
            pool_t[h, :, xl] = turned[xl * 256 : (xl + 1) * 256, :].reshape(8, 32, 128)
    rows_came = spray(
        2, grp_dev,
        lambda j: pool_t.at[lax.rem(i + j, 2), lax.rem(i + j, 16) // 2], lambda j: pool_rows.at[i], pool_rows,
    )

    rhs_all[...] = jnp.zeros((2048, 256), BF16)

    tot_came.wait()
    acc = tot_a[0]
    for s in range(1, 8):
        acc = acc + tot_a[s]
    tot_own[1] = acc
    tot_came = spray(4, xy_dev, lambda j: tot_own.at[1], lambda j: tot_b.at[g], tot_b)

    inv_p = 1.0 / p_norm
    tot_came.wait()
    acc = tot_b[0]
    for s in range(1, 16):
        acc = acc + tot_b[s]
    totals = acc[:, 0:256]
    coeff = 50.0 * (expo / totals - target)

    def v1_part(order, j, part):
        to = lax.rem(here(order) + j, 4)
        return v1.at[0, to, part] if order == 0 else v1.at[1, part, to]

    def ring(order, side, n):
        return (vb1 if order else va1).at[n + (0 if side == 1 else 3)]

    def ring_sem(order, side, n):
        return (49 if side == 1 else 42) + n + (4 if order and side == 1 else 3 if order else 0)

    by_p = jnp.transpose(jnp.concatenate([coeff * inv_p, jnp.zeros((64, 256), F32)], axis=0))[:, 0:64].astype(BF16)
    for order in range(2):
        for n in range(2):
            cols = pl.ds(pl.multiple_of(core * HALF + (order * QCOL + n * 512), 512), 512)
            part = dot(by_p, p_all[:, :, cols].reshape(64, 512), 1, 0)
            v1[order, :, :, :, n * 512 : (n + 1) * 512] = part.astype(BF16).reshape(4, 4, 16, 512)
        for side, part, rest in ((1, low, high), (3, high, low)):
            send(v1_part(order, 2, part), ring(order, side, 0), ring_sem(order, side, 0), along(order, side))
            send(v1_part(order, side, rest), ring(order, side, 1), ring_sem(order, side, 1), along(order, side))

    def own_rows(rows):
        return jnp.where(core == 0, rows[0:32], rows[32:64])

    by_q = (own_rows(coeff) / q_norm).astype(BF16)
    radial = own_rows(jnp.sum(coeff * cosine, axis=1, keepdims=True) * inv_p)
    inv_own = own_rows(inv_p)
    for n in range(4):
        cols = slice(n * QCOL, (n + 1) * QCOL)
        p_sum = dot(by_q, q_block_of(n // 2, n % 2), 1, 0)
        pg[:, cols] = (p_sum - p_all[core, :, cols].astype(F32) * radial) * inv_own
    out_p = pltpu.make_async_copy(pg, passage_out, out_sem.at[0])
    out_p.start()

    def ring_on(order):
        for side, part in ((1, low), (3, high)):
            arrived(ring(order, side, 0), ring_sem(order, side, 0))
            added = v1_part(order, side, part)[...].astype(F32) + ring(order, side, 0)[...].astype(F32)
            slot = order * 2 + (0 if side == 1 else 1)
            v_fwd[slot] = added.astype(BF16)
            send(v_fwd.at[slot], ring(order, side, 2), ring_sem(order, side, 2), along(order, side))

    def ring_end(order):
        second = v2b if order else v2a
        for side in (1, 3):
            for n in (1, 2):
                arrived(ring(order, side, n), ring_sem(order, side, n))
        for part, side in ((low, 1), (high, 3)):
            piece = v1_part(order, 0, part)[...].astype(F32)
            piece = piece + ring(order, side, 2)[...].astype(F32)
            piece = piece + ring(order, 4 - side, 1)[...].astype(F32)
            second[part] = piece.astype(BF16)
        for j in range(1, 4):
            if order == 0:
                send(v2a.at[lax.rem(y + j, 4)], va2.at[j - 1], 56 + j, y_dev(j))
            else:
                send(v2b.at[lax.rem(x + j, 4)], vb2.at[j - 1], 60 + j, x_dev(j))

    for r in range(32):
        rows32[r : r + 1, :] = pg[0:1, r * 128 : (r + 1) * 128]
    l_gf.wait()
    upstream = rows32[...] * gf_in[...]
    mean_uf = total(upstream * final) * (1.0 / D)
    dstate = oscale * (upstream - final * (oscale * oscale) * mean_uf)
    s_own[0] = dstate[0:16, :].astype(BF16)
    s_own[1] = dstate[16:32, :].astype(BF16)
    send(s_own.at[other], d_sib, 28, sibling)
    s_came = spray(5, grp_dev, lambda j: s_own.at[lax.rem(i + j, 2)], lambda j: s_all.at[y, i], s_all.at[y])

    ring_on(0)
    ring_on(1)

    arrived(d_sib, 28)
    head16 = (lax.broadcasted_iota(jnp.int32, (32, 512), 0) & 15) >> 2
    kv16 = lax.broadcasted_iota(jnp.int32, (32, 512), 1) >> 7
    both_d = jnp.concatenate([jnp.where(core == 0, dstate[0:16], dstate[16:32]), d_sib[...].astype(F32)], axis=0)
    both_d = jnp.where(head16 == kv16, jnp.concatenate([both_d] * 4, axis=1), 0.0).astype(BF16)
    my_kv = pl.ds(pl.multiple_of(core * 512, 512), 512)

    def spread_piece(n):
        cols = slice(n * 512, (n + 1) * 512)
        piece = (dot(both_d, wv_in[cols, my_kv], 1, 1) * ga_in[:, cols]).astype(BF16)
        spread[core, :, cols] = piece[0:16, :]
        g_own[n // 4, :, (n % 4) * 512 : (n % 4 + 1) * 512] = piece[16:32, :]
        if n % 4 == 3:
            dst = spread.at[core, :, pl.ds((n // 4) * HALF, HALF)]
            send(g_own.at[n // 4], dst, 48 + 8 * (n // 4), sibling)

    for n in range(0, 4):
        spread_piece(n)
    ring_end(0)
    ring_end(1)

    s_came.wait()
    for j in range(1, 4):
        send(s_all.at[y], s_all.at[y], 28 + j, y_dev(j))

    for n in range(4, 8):
        spread_piece(n)

    rows_came.wait()
    lane_kv = (lax.broadcasted_iota(jnp.int32, (64, 128), 1) & 15) >> 2
    for s in range(16):
        rows = pool_rows[s].reshape(64, 128).astype(F32)
        for k in range(4):
            lhs_all[k * 64 : (k + 1) * 64, s * 128 : (s + 1) * 128] = jnp.where(lane_kv == k, rows, 0.0).astype(BF16)

    for j in range(1, 4):
        arrived(va2.at[j - 1], 56 + j)
        arrived(vb2.at[j - 1], 60 + j)
    acc_a = v2a[y].astype(F32)
    acc_b = v2b[x].astype(F32)
    for j in range(3):
        acc_a = acc_a + va2[j].astype(F32)
        acc_b = acc_b + vb2[j].astype(F32)
    pieces = [acc_a[:, j * 128 : (j + 1) * 128] for j in range(8)]
    pieces += [acc_b[:, j * 128 : (j + 1) * 128] for j in range(8)]
    stacked = jnp.concatenate([piece.astype(BF16) for piece in pieces], axis=0)
    v3[...] = dot(perm[...], stacked, 1, 0).astype(BF16).reshape(16, 16, 128)
    v3_came = spray(6, grp_dev, lambda j: v3.at[lax.rem(i + j, 16)], lambda j: v3_recv.at[i], v3_recv)

    for j in range(1, 4):
        arrived(s_all.at[lax.rem(y + 4 - j, 4)], 28 + j)
    for s in range(16):
        block = s_all[:, s].reshape(64, 128)
        rhs_all[s * 128 : s * 128 + 64, 0:128] = block
        rhs_all[s * 128 + 64 : (s + 1) * 128, 128:256] = block
    grads = dot(lhs_all[...], rhs_all[...], 1, 0).astype(BF16)
    for to in range(8):
        xp, xl, cr = to // 4, (to // 2) % 2, to % 2
        for k in range(4):
            first = k * 64 + xl * 32 + cr * 16
            w_send[xp * 2 + xl, cr, :, k * 128 : (k + 1) * 128] = grads[
                first : first + 16, xp * 128 : (xp + 1) * 128
            ]
    for j in range(1, 4):
        send(w_send.at[lax.rem(x + j, 4), core], w_recv.at[x, core], 32 + j, x_dev(j))
        send(w_send.at[lax.rem(x + j, 4), other], w_recv.at[x, core], 36 + j, x_far(j))
    send(w_send.at[x, other], w_recv.at[x, core], 36, sibling)
    keep_w = pltpu.make_async_copy(w_send.at[x, core], w_recv.at[x, core], one_recv.at[32])
    keep_w.start()

    drow[...] = jnp.zeros((16, D), F32)
    for r in range(32):
        drow[0:1, r * 128 : (r + 1) * 128] = dstate[r : r + 1, :]
    spread[2] = drow[...].astype(BF16)
    for n in range(2):
        arrived(spread.at[other, :, pl.ds(n * HALF, HALF)], 48 + 8 * n)
    mix = dot(spread[0:2].reshape(32, D), h_in[...], 1, 1)
    mean_row = jnp.sum(weights * mix, axis=0, keepdims=True) * (rs_row * rs_row * rs_row) * (1.0 / D)
    mean_all = jnp.transpose(jnp.broadcast_to(mean_row, (128, 256)))

    loss = total(jnp.log(totals) + 50.0 - acc[:, 256:512]) * (1.0 / 256.0)
    loss_out[...] = jnp.broadcast_to(loss, (1, 128))

    def hidden_rows(b):
        rows = slice(b * 128, (b + 1) * 128)
        for n in range(8):
            cols = slice(n * 512, (n + 1) * 512)
            grad = dot(wts_t[rows, :], spread[:, :, cols].reshape(48, 512), 1, 0)
            scale = jnp.concatenate([mean_all[rows]] * 4, axis=1)
            hg[b, :, cols] = (grad - h_in[rows, cols].astype(F32) * scale).astype(BF16)
        copy = pltpu.make_async_copy(hg.at[b], hidden_out.at[pl.ds(b * 128, 128)], out_sem.at[1 + b])
        copy.start()
        return copy

    out_h = [hidden_rows(0), hidden_rows(1)]

    keep_w.wait()
    arrived(w_recv.at[x, other], 36)
    for j in range(1, 4):
        arrived(w_recv.at[lax.rem(x + 4 - j, 4), core], 32 + j)
        arrived(w_recv.at[lax.rem(x + 4 - j, 4), other], 36 + j)
    for h in range(2):
        acc_w = w_recv[0, h].astype(F32)
        for s in range(1, 4):
            acc_w = acc_w + w_recv[s, h].astype(F32)
        wg[:, h * 512 : (h + 1) * 512] = acc_w
    out_w = pltpu.make_async_copy(wg, weight_out, out_sem.at[3])
    out_w.start()

    for copy in sends:
        copy.wait_send()
    for wait in sprays:
        wait.wait()
    v3_came.wait()
    halves = []
    for h in range(2):
        acc_q = v3_recv[h].astype(F32)
        for s in range(1, 8):
            acc_q = acc_q + v3_recv[2 * s + h].astype(F32)
        halves.append(acc_q)
    q_sum = jnp.concatenate(halves, axis=0)
    own = q_rows[...]
    own_square = total(own * own) + 1e-06
    own_dot = total(own * q_sum)
    qg[...] = (q_sum - own * (own_dot / own_square)) * lax.rsqrt(own_square)
    out_q = pltpu.make_async_copy(qg, query_out, out_sem.at[4])
    out_q.start()
    out_p.wait()
    for copy in out_h:
        copy.wait()
    out_w.wait()
    out_q.wait()


def hand_on(
    l_in, q_in, p_in, w_in, h_in, l_out, q_out, p_out, w_out, h_out, l_via, q_via, p_via, w_via, h_via, sem_in, sem_out
):
    steps = [(l_in, l_via, l_out), (q_in, q_via, q_out), (w_in, w_via, w_out), (p_in, p_via, p_out)]
    for n in range(4):
        rows = pl.ds(n * 64, 64)
        steps.append((h_in.at[rows], h_via.at[rows], h_out.at[rows]))
    loads = [pltpu.make_async_copy(src, via, sem_in.at[n]) for n, (src, via, _) in enumerate(steps)]
    stores = [pltpu.make_async_copy(via, dst, sem_out.at[n]) for n, (_, via, dst) in enumerate(steps)]
    for load in loads:
        load.start()
    for load, store in zip(loads, stores):
        load.wait()
        store.start()
    for store in stores:
        store.wait()


def per_device(
    queries, passages, positives, hidden, gain_attn, value_weight, keys, last_query, lengths, gain_final
):
    anywhere = pl.BlockSpec(memory_space=pl.ANY)
    vmem = pltpu.VMEM
    dma = pltpu.SemaphoreType.DMA
    scratch = [
        pltpu.SMEM((1,), jnp.int32), vmem((1, D), BF16), vmem((2, 32, D), BF16), vmem((1, 256), jnp.int32), vmem((SEQ, D), BF16),
        vmem((1, D), F32), vmem((D, KVW), BF16), vmem((SEQ, KVW), BF16), vmem((1, D), BF16),
        vmem((32, 128), F32),
        vmem((256, 256), BF16), vmem((32, 128), F32), vmem((32, 128), F32), vmem((2, 16, 128), BF16),
        vmem((16, 16, 128), BF16), vmem((2, 4, 4, 16, QCOL), BF16), vmem((2, 4, 4, 16, BCOL), BF16), vmem((2, 16, 128), BF16),
        vmem((4, 16, 16, 128), BF16),
        vmem((2, 1, 512), F32), vmem((8, 1, 512), F32), vmem((16, 1, 512), F32), vmem((4, 2, 16, 1024), BF16),
        vmem((4, 2, 16, 1024), BF16), vmem((2, 8, 2, 32, 128), BF16), vmem((16, 2, 32, 128), BF16),
        vmem((256, 2048), BF16), vmem((2048, 256), BF16), vmem((4, 2, 16, 512), BF16), vmem((4, 2, 16, 512), BF16),
        vmem((48, SEQ), BF16), vmem((SEQ, 128), F32), vmem((32, D), F32), vmem((3, 16, D), BF16),
        vmem((16, D), F32), vmem((2, 128, D), BF16),
        vmem((32, D), BF16), vmem((SEQ, 48), BF16), vmem((2, 16, HALF), BF16), vmem((16, 128), BF16),
        vmem((2, 4, 4, 16, QCOL), BF16), vmem((6, 2, 16, QCOL), BF16), vmem((6, 2, 16, QCOL), BF16),
        vmem((4, 2, 16, QCOL), BF16),
        vmem((4, 16, QCOL), BF16), vmem((4, 16, QCOL), BF16), vmem((3, 16, QCOL), BF16),
        vmem((3, 16, QCOL), BF16), vmem((16, 16, 128), BF16), vmem((16, 16, 128), BF16),
        vmem((16, KVW), F32), vmem((32, 128), F32),
        dma((10,)), dma((5,)), dma((7,)), dma((7,)), dma((64,)), dma((64,)), dma((1,)),
    ]
    loss, query_grad, passage_grad, weight_grad, hidden_grad = pl.pallas_call(
        kernel,
        out_shape=(
            jax.ShapeDtypeStruct((1, 128), F32),
            jax.ShapeDtypeStruct((32, 128), F32),
            jax.ShapeDtypeStruct((32, D), F32),
            jax.ShapeDtypeStruct((16, KVW), F32),
            jax.ShapeDtypeStruct((SEQ, D), BF16),
        ),
        in_specs=[anywhere] * 10,
        out_specs=(pl.BlockSpec(memory_space=pltpu.VMEM),) + (anywhere,) * 4,
        scratch_shapes=scratch,
        compiler_params=pltpu.CompilerParams(
            collective_id=0, has_side_effects=True, vmem_limit_bytes=56 * 1024 * 1024
        ),
    )(
        lengths, queries, passages, positives.reshape(1, 256), hidden.reshape(SEQ, D),
        gain_attn.reshape(1, D), value_weight, keys.reshape(SEQ, KVW), last_query,
        gain_final.reshape(32, 128),
    )
    grads = (loss, query_grad, passage_grad, weight_grad, hidden_grad)
    loss, query_grad, passage_grad, weight_grad, hidden_grad = pl.pallas_call(
        hand_on,
        out_shape=tuple(jax.ShapeDtypeStruct(leaf.shape, leaf.dtype) for leaf in grads),
        in_specs=[anywhere] * 5,
        out_specs=(anywhere,) * 5,
        scratch_shapes=[vmem(leaf.shape, leaf.dtype) for leaf in grads] + [dma((8,)), dma((8,))],
        compiler_params=pltpu.CompilerParams(vmem_limit_bytes=56 * 1024 * 1024),
    )(*grads)
    return (loss[0, 0], query_grad.reshape(1, D), passage_grad, weight_grad, hidden_grad.reshape(1, SEQ, D))


def solution(mesh):
    placed = (
        P("dp", None),
        P("dp", None),
        P(),
        P("dp", None, None),
        P(),
        P(),
        P("dp", None, None),
        P("dp", None),
        P("dp"),
        P(),
    )
    return jax.shard_map(
        per_device,
        mesh=mesh,
        in_specs=placed,
        out_specs=(P(), P("dp", None), P("dp", None), P("dp", None), P("dp", None, None)),
        check_vma=False,
    )
```
